32 devices in a mesh: src: 32 (over z, y, x, core), dst: 1.
Axes of the slice: x: 2, y: 2, z: 4, core: 2. Of those that a mesh axis runs over, the one named last changes fastest.
Arguments:
- out_density: float32 [16384], P('src'), may hold values from 0.008 to 0.08
- in_density: float32 [16384], P('dst'), may hold values from 0.008 to 0.08
- retention: float32 [16384], P('src'), may hold values from 0.15 to 0.75
- demand: float32 [16384], P('src'), may hold values from 0.5 to 4
- location: int32 [16384], replicated, may hold values from 0 to 16383
- scenario_blocks: int32 [32], replicated, may hold values from 0 to 127
Outputs:
- out_fitness: float32 [16384], P('src')
- in_fitness: float32 [16384], P('dst')
- levels: float32 [16384, 32], P('src', 'dst')
The draws below stay inside these ranges and needn't reach their ends.
Inputs may be any that keep to these rules, and one draw needn't show every extreme that they name: `scenario_blocks`: scenario k extracts the 128 firms of block index b = scenario_blocks_k, firms 128 * b to 128 * b + 127. `location`: several firms may share a map cell, and some cells hold none.
All inputs are finite; a program needn't handle non-finite values.
Results may differ from the reference program's by a relative error of at most 0.0003.
Values sent between devices are 32-bit elements; how exact they have to be, the bound alone decides.
A program may use at most 64 MiB of HBM per device.

```python
import math
import jax
import jax.numpy as jnp
from jax import lax

SCEN = 32
SWEEPS = 2
ITERS = 2
EXTRACT = 128
MAP_SIDE = 256
RANGE = 18
FIRMS = 16384


def set_ends(entries, stream_key, low, top_value):
    dims = entries.shape
    place = [jax.random.randint(jax.random.fold_in(stream_key, axis), (), 0, dims[axis]) for axis in range(len(dims))]
    entries = entries.at[tuple(place)].set(low)
    longest = dims.index(max(dims))
    place[longest] = (place[longest] + 1) % dims[longest]
    return entries.at[tuple(place)].set(top_value)


def block_scale(stream_key, shape, cuts, smallest, high):
    def one(axis_at, blocks):
        steps = jax.random.uniform(jax.random.fold_in(jax.random.fold_in(stream_key, 6), axis_at), (blocks,), jnp.float32, smallest / len(cuts), high / len(cuts))
        return jnp.repeat(jnp.exp(steps), shape[axis_at] // blocks).reshape((-1,) + (1,) * (len(shape) - axis_at - 1))

    level = one(*cuts[0])
    for cut in cuts[1:]:
        level = level * one(*cut)
    return level


def setup_inputs(seed: int = 0) -> dict:
    keys = jax.random.split(jax.random.key(seed), 7)
    out_density = jnp.clip(jnp.exp(math.log(0.08) - 2.30258502 * jax.random.uniform(keys[0], (FIRMS,), jnp.float32) ** block_scale(keys[0], (FIRMS,), ((0, 32),), -0.2, 0.2)), 0.008, 0.08)
    in_density = jnp.clip(jnp.exp(jax.random.uniform(keys[1], (FIRMS,), jnp.float32, math.log(0.008), math.log(0.08))), 0.008, 0.08)
    retention = jnp.clip(jnp.exp(math.log(0.75) - 1.60943787 * jax.random.uniform(keys[2], (FIRMS,), jnp.float32) ** block_scale(keys[2], (FIRMS,), ((0, 32),), -0.2, 0.2)), 0.15, 0.75)
    demand = jnp.clip(jnp.exp(math.log(4.0) - 2.0794415 * jax.random.uniform(keys[3], (FIRMS,), jnp.float32) ** block_scale(keys[3], (FIRMS,), ((0, 32),), -0.2, 0.2)), 0.5, 4.0)
    location = set_ends(jax.random.randint(keys[4], (FIRMS,), 0, FIRMS), jax.random.fold_in(keys[4], 1), 0, FIRMS - 1).astype(jnp.int32)
    scenario_blocks = set_ends(jax.random.randint(keys[5], (SCEN,), 0, FIRMS // EXTRACT), jax.random.fold_in(keys[5], 1), 0, (FIRMS // EXTRACT) - 1).astype(jnp.int32)
    return {"out_density": out_density, "in_density": in_density, "retention": retention, "demand": demand, "location": location, "scenario_blocks": scenario_blocks}


far_weight = 0.015625

def reference(out_density, in_density, retention, demand, location, scenario_blocks):
    height = math.gcd(FIRMS, 512)
    blocks = FIRMS // height
    firm_ids = jnp.arange(FIRMS, dtype=jnp.int32)
    offsets = jnp.arange(blocks, dtype=jnp.int32) * height
    map_row = (location // MAP_SIDE).astype(jnp.int32)
    map_col = (location % MAP_SIDE).astype(jnp.int32)
    out_fit = jnp.sqrt(out_density)
    in_fit = jnp.sqrt(in_density)

    def pair_weight(offset):
        row_ids = offset + jnp.arange(height, dtype=jnp.int32)
        row_gap = lax.dynamic_slice_in_dim(map_row, offset, height)[:, None] - map_row[None, :]
        col_gap = lax.dynamic_slice_in_dim(map_col, offset, height)[:, None] - map_col[None, :]
        nearby = row_gap * row_gap + col_gap * col_gap <= RANGE * RANGE
        affinity = jnp.where(nearby, 1.0, far_weight)
        return jnp.where(row_ids[:, None] != firm_ids[None, :], affinity, 0.0)
    for sweep_no in range(SWEEPS):

        def row_part(offset):
            row_fit = lax.dynamic_slice_in_dim(out_fit, offset, height)
            weight = pair_weight(offset)
            ratios = weight * in_fit[None, :] / (1.0 + row_fit[:, None] * in_fit[None, :] * weight)
            return lax.optimization_barrier(jnp.sum(ratios, axis=1))
        row_total = lax.map(row_part, offsets).reshape(FIRMS)
        out_fit = FIRMS * out_density / row_total

        def col_part(running, offset):
            row_fit = lax.dynamic_slice_in_dim(out_fit, offset, height)
            weight = pair_weight(offset)
            ratios = weight * row_fit[:, None] / (1.0 + row_fit[:, None] * in_fit[None, :] * weight)
            return (running + lax.optimization_barrier(jnp.sum(ratios, axis=0)), None)
        col_total, _ = lax.scan(col_part, jnp.zeros((FIRMS,), out_fit.dtype), offsets)
        in_fit = FIRMS * in_density / col_total
    row_scale = retention / (FIRMS * out_density)
    retained = (firm_ids[:, None] // EXTRACT != scenario_blocks[None, :]).astype(jnp.float32)
    levels = retained * demand[:, None]
    for round_no in range(ITERS):
        current = levels

        def product_part(offset):
            row_fit = lax.dynamic_slice_in_dim(out_fit, offset, height)
            scale_part = lax.dynamic_slice_in_dim(row_scale, offset, height)
            product = row_fit[:, None] * in_fit[None, :] * pair_weight(offset)
            chance = product / (1.0 + product)
            coeff = chance * scale_part[:, None]
            return jnp.dot(coeff, current, preferred_element_type=jnp.float32, precision=lax.Precision.HIGHEST)
        summed = lax.map(product_part, offsets).reshape(FIRMS, SCEN)
        levels = retained * (demand[:, None] + summed)
    return (out_fit, in_fit, levels)
```

```python
import functools
import math

import jax
import jax.numpy as jnp
from jax import lax
from jax.experimental import pallas as pl
from jax.experimental.pallas import tpu as pltpu
from jax.sharding import PartitionSpec as P

SWEEPS = 2
ITERS = 2
EXTRACT = 128
MAP_SIDE = 256
RANGE = 18


far_weight = 0.015625
FAR = 64.0
ROWS = 64
LANES = 128


def kernel(
    n,
    left_ref,
    right_ref,
    od_ref,
    ret_ref,
    dem_ref,
    dem_row_ref,
    ind_ref,
    scen_ref,
    x_out,
    y_out,
    lev_out,
    bmat,
    hi_ref,
    lo_ref,
    rowacc,
    xb,
    vb,
    part,
    gath,
    yrow,
    urow,
    dem_all,
    lev_all,
    acc,
    send_sem,
    one_sem,
    lev_sem,
):
    me = lax.axis_index("src")
    rows, cols = bmat.shape
    firms = rows * n
    scen = scen_ref.shape[0]
    wide = rows // LANES

    barrier = pltpu.get_barrier_semaphore()

    @pl.loop(1, n)
    def _(s):
        pl.semaphore_signal(barrier, inc=1, device_id={"src": lax.rem(me + s, n)})

    pl.semaphore_wait(barrier, n - 1)

    def push(src, dst, sems, phase):
        @pl.loop(1, n)
        def _(s):
            q = lax.rem(me + n - s, n)
            pltpu.make_async_remote_copy(
                src_ref=src(q),
                dst_ref=dst.at[me],
                send_sem=send_sem.at[phase],
                recv_sem=sems,
                device_id={"src": q},
            ).start()

    def drain(buf, sem):
        some = buf.at[pl.ds(0, n - 1)]
        pltpu.make_async_copy(some, some, sem).wait()

    dem_all[me] = dem_row_ref[...]
    push(lambda q: dem_row_ref, dem_all, one_sem.at[0], 0)

    @pl.loop(0, n)
    def _(q):
        c0 = pl.multiple_of(q * rows, rows)
        dist = jnp.dot(
            left_ref[...],
            right_ref[:, pl.ds(c0, rows)],
            preferred_element_type=jnp.float32,
        )
        bmat[:, pl.ds(c0, rows)] = jnp.where(dist <= RANGE * RANGE, 1.0, FAR)

    mine = pl.ds(pl.multiple_of(me * rows, rows), rows)
    for r0 in range(0, rows, ROWS):
        shape = (ROWS, rows)
        same = lax.broadcasted_iota(jnp.int32, shape, 0) + r0 == lax.broadcasted_iota(
            jnp.int32, shape, 1
        )
        bmat[pl.ds(r0, ROWS), mine] = jnp.where(same, jnp.inf, bmat[pl.ds(r0, ROWS), mine])

    xb[...] = jnp.broadcast_to(jnp.sqrt(od_ref[...]), xb.shape)

    @pl.loop(0, n)
    def _(q):
        c0 = pl.multiple_of(q * rows, rows)
        y = jnp.sqrt(ind_ref[q])
        yrow[:, pl.ds(c0, rows)] = y
        urow[:, pl.ds(c0, rows)] = 1.0 / y

    tiles = 16
    strip = tiles * LANES
    for sweep in range(SWEEPS):
        @pl.loop(0, rows // ROWS)
        def _(b):
            rs = pl.ds(pl.multiple_of(b * ROWS, ROWS), ROWS)
            x = xb[rs, :]

            def body(c, total):
                c0 = pl.multiple_of(c * strip, strip)
                for t in range(tiles):
                    cs = pl.ds(c0 + t * LANES, LANES)
                    total = total + pl.reciprocal(bmat[rs, cs] * urow[:, cs] + x, approx=True)
                return total

            rowacc[rs, :] = lax.fori_loop(
                0, cols // strip, body, jnp.zeros((ROWS, LANES), jnp.float32)
            )

        row_total = jnp.sum(rowacc[...], axis=1, keepdims=True)
        x_new = firms * od_ref[...] / row_total
        xb[...] = jnp.broadcast_to(x_new, xb.shape)
        vb[...] = jnp.broadcast_to(1.0 / x_new, vb.shape)

        @pl.loop(0, n)
        def _(q):
            c0 = pl.multiple_of(q * rows, rows)
            for t in range(wide):
                cs = pl.ds(c0 + t * LANES, LANES)
                y = yrow[:, cs]
                total = jnp.zeros((8, LANES), jnp.float32)
                for r0 in range(0, rows, ROWS):
                    rs = pl.ds(r0, ROWS)
                    term = pl.reciprocal(bmat[rs, cs] * vb[rs, :] + y, approx=True)
                    total = total + jnp.sum(term.reshape(ROWS // 8, 8, LANES), axis=0)
                part[sweep, q, :, pl.ds(t * LANES, LANES)] = jnp.sum(total, axis=0, keepdims=True)

        gath[2 * sweep, me] = part[sweep, me]
        push(lambda q: part.at[sweep, q], gath.at[2 * sweep], one_sem.at[1 + 2 * sweep], 1 + 2 * sweep)
        drain(gath.at[2 * sweep], one_sem.at[1 + 2 * sweep])
        col_total = jnp.sum(gath[2 * sweep], axis=0)
        fresh = gath.at[2 * sweep + 1]
        fresh[me] = firms * ind_ref[me] / col_total
        push(lambda q: fresh.at[me], fresh, one_sem.at[2 + 2 * sweep], 2 + 2 * sweep)
        drain(fresh, one_sem.at[2 + 2 * sweep])

        @pl.loop(0, n)
        def _(q):
            c0 = pl.multiple_of(q * rows, rows)
            y = fresh[q]
            yrow[:, pl.ds(c0, rows)] = y
            urow[:, pl.ds(c0, rows)] = 1.0 / y

    y_out[...] = gath[2 * SWEEPS - 1]
    x_new = xb[:, 0:1]
    x_out[...] = x_new
    gain = x_new * (ret_ref[...] / (firms * od_ref[...]))
    drain(dem_all, one_sem.at[0])

    def kept(q):
        ids = q * rows + lax.broadcasted_iota(jnp.int32, (scen, rows), 1)
        return lax.div(ids, EXTRACT) != scen_ref[...]

    def product(levels):
        top = levels.astype(jnp.bfloat16)
        low = (levels - top.astype(jnp.float32)).astype(jnp.bfloat16)
        both = jnp.concatenate([top, low], axis=0)
        dims = (((1,), (1,)), ((), ()))
        acc[...] += lax.dot_general(
            hi_ref[...], both, dims, preferred_element_type=jnp.float32
        ) + lax.dot_general(lo_ref[...], both, dims, preferred_element_type=jnp.float32)

    def split(rs, value):
        top = value.astype(jnp.bfloat16)
        hi_ref[rs, :] = top
        lo_ref[rs, :] = (value - top.astype(jnp.float32)).astype(jnp.bfloat16)

    acc[...] = jnp.zeros_like(acc)

    @pl.loop(0, n)
    def _(q):
        cs = pl.ds(pl.multiple_of(q * rows, rows), rows)
        u = urow[:, cs]
        for r0 in range(0, rows, ROWS):
            rs = pl.ds(r0, ROWS)
            x = jnp.concatenate([xb[rs, :]] * wide, axis=1)
            value = pl.reciprocal(bmat[rs, cs] * u + x, approx=True)
            bmat[rs, cs] = value
            split(rs, value)
        product(jnp.where(kept(q), dem_all[q], 0.0))

    summed = gain * (acc[:, 0:scen] + acc[:, scen:])
    keep_mine = kept(me)
    fresh_levels = jnp.where(keep_mine, dem_row_ref[...] + summed.T, 0.0)
    lev_all[me] = fresh_levels
    acc[...] = jnp.zeros_like(acc)
    lev_mine = lev_all.at[me]

    @pl.loop(1, n)
    def _(s):
        q = lax.rem(me + n - s, n)
        pltpu.make_async_remote_copy(
            src_ref=lev_mine,
            dst_ref=lev_all.at[me],
            send_sem=send_sem.at[5],
            recv_sem=lev_sem.at[me],
            device_id={"src": q},
        ).start()

    @pl.loop(0, n)
    def _(s):
        q = lax.rem(me + s, n)
        cs = pl.ds(pl.multiple_of(q * rows, rows), rows)
        for r0 in range(0, rows, ROWS):
            rs = pl.ds(r0, ROWS)
            split(rs, bmat[rs, cs])

        @pl.when(s > 0)
        def _():
            slot = lev_all.at[q]
            pltpu.make_async_copy(slot, slot, lev_sem.at[q]).wait()

        product(lev_all[q])

    summed = gain * (acc[:, 0:scen] + acc[:, scen:])
    ids = me * rows + lax.broadcasted_iota(jnp.int32, (scen, rows), 1)
    lev_out[...] = jnp.where(keep_mine, dem_row_ref[...] + summed.T, 0.0).T

    drain(dem_all, send_sem.at[0])
    for phase in range(1, 5):
        drain(gath.at[0], send_sem.at[phase])
    drain(lev_all, send_sem.at[5])


def fused(out_density, in_density, retention, demand, location, scenario_blocks):
    rows = out_density.shape[0]
    cols = in_density.shape[0]
    n = lax.axis_size("src")
    scen = scenario_blocks.shape[0]
    mine = lax.dynamic_slice_in_dim(location, lax.axis_index("src") * rows, rows)

    def bytes_of(norm):
        return norm >> 16, (norm >> 8) & 255, norm & 255

    def features(cells, left):
        r, c = cells // MAP_SIDE, cells % MAP_SIDE
        norm = bytes_of(r * r + c * c)
        one = jnp.ones_like(r)
        scale = (65536 * one, 256 * one, one)
        head = (-2 * r, -2 * c) if left else (r, c)
        tail = norm + scale if left else scale + norm
        zero = jnp.zeros_like(r)
        return jnp.stack(head + tail + (zero,) * 8, axis=1 if left else 0).astype(jnp.bfloat16)

    vmem = pl.BlockSpec(memory_space=pltpu.VMEM)
    f32 = jnp.float32
    x, y, levels = pl.pallas_call(
        functools.partial(kernel, n),
        out_shape=(
            jax.ShapeDtypeStruct((rows, 1), f32),
            jax.ShapeDtypeStruct((n, 1, rows), f32),
            jax.ShapeDtypeStruct((rows, scen), f32),
        ),
        in_specs=[vmem] * 8,
        out_specs=(vmem,) * 3,
        scratch_shapes=[
            pltpu.VMEM((rows, cols), f32),
            pltpu.VMEM((rows, rows), jnp.bfloat16),
            pltpu.VMEM((rows, rows), jnp.bfloat16),
            pltpu.VMEM((rows, LANES), f32),
            pltpu.VMEM((rows, LANES), f32),
            pltpu.VMEM((rows, LANES), f32),
            pltpu.VMEM((SWEEPS, n, 1, rows), f32),
            pltpu.VMEM((2 * SWEEPS, n, 1, rows), f32),
            pltpu.VMEM((1, cols), f32),
            pltpu.VMEM((1, cols), f32),
            pltpu.VMEM((n, 1, rows), f32),
            pltpu.VMEM((n, scen, rows), f32),
            pltpu.VMEM((rows, 2 * scen), f32),
            pltpu.SemaphoreType.DMA((6,)),
            pltpu.SemaphoreType.DMA((5,)),
            pltpu.SemaphoreType.DMA((n,)),
        ],
        compiler_params=pltpu.CompilerParams(
            collective_id=0, has_side_effects=True, vmem_limit_bytes=56 * 2**20
        ),
    )(
        features(mine, True),
        features(location, False),
        out_density[:, None],
        retention[:, None],
        demand[:, None],
        demand[None, :],
        in_density.reshape(n, 1, rows),
        scenario_blocks[:, None],
    )
    return x.reshape(rows), y.reshape(cols), levels


def on_device(out_density, in_density, retention, demand, location, scenario_blocks):
    rows_dev = out_density.shape[0]
    cols_dev = in_density.shape[0]
    firms = rows_dev * lax.axis_size("src")
    row_start = lax.axis_index("src") * rows_dev
    col_start = lax.axis_index("dst") * cols_dev
    height = math.gcd(rows_dev, 128)
    blocks = rows_dev // height
    col_ids = col_start + jnp.arange(cols_dev, dtype=jnp.int32)
    offsets = jnp.arange(blocks, dtype=jnp.int32) * height
    src_cells = lax.dynamic_slice_in_dim(location, row_start, rows_dev)
    dst_cells = lax.dynamic_slice_in_dim(location, col_start, cols_dev)
    src_row = src_cells // MAP_SIDE
    src_col = src_cells % MAP_SIDE
    dst_row = dst_cells // MAP_SIDE
    dst_col = dst_cells % MAP_SIDE
    out_fit = jnp.sqrt(out_density)
    in_fit = jnp.sqrt(in_density)

    def pair_weight(offset):
        row_ids = row_start + offset + jnp.arange(height, dtype=jnp.int32)
        row_gap = lax.dynamic_slice_in_dim(src_row, offset, height)[:, None] - dst_row[None, :]
        col_gap = lax.dynamic_slice_in_dim(src_col, offset, height)[:, None] - dst_col[None, :]
        nearby = row_gap * row_gap + col_gap * col_gap <= RANGE * RANGE
        affinity = jnp.where(nearby, 1.0, far_weight)
        return jnp.where(row_ids[:, None] != col_ids[None, :], affinity, 0.0)

    for sweep_no in range(SWEEPS):

        def row_part(offset):
            row_fit = lax.dynamic_slice_in_dim(out_fit, offset, height)
            weight = pair_weight(offset)
            ratios = weight * in_fit[None, :] / (1.0 + row_fit[:, None] * in_fit[None, :] * weight)
            return jnp.sum(ratios, axis=1)

        row_partial = lax.map(row_part, offsets).reshape(rows_dev)
        row_total = lax.psum(row_partial, "dst")
        out_fit = firms * out_density / row_total

        def col_part(running, offset):
            row_fit = lax.dynamic_slice_in_dim(out_fit, offset, height)
            weight = pair_weight(offset)
            ratios = weight * row_fit[:, None] / (1.0 + row_fit[:, None] * in_fit[None, :] * weight)
            return (running + jnp.sum(ratios, axis=0), None)

        col_partial, _ = lax.scan(col_part, jnp.zeros((cols_dev,), jnp.float32), offsets)
        col_total = lax.psum(col_partial, "src")
        in_fit = firms * in_density / col_total
    row_scale = retention / (firms * out_density)

    def coeff_block(offset):
        row_fit = lax.dynamic_slice_in_dim(out_fit, offset, height)
        scale_part = lax.dynamic_slice_in_dim(row_scale, offset, height)
        product = row_fit[:, None] * in_fit[None, :] * pair_weight(offset)
        chance = product / (1.0 + product)
        return chance * scale_part[:, None]

    coefficients = lax.map(coeff_block, offsets).reshape(rows_dev, cols_dev)
    scenarios = scenario_blocks.shape[0]
    portion = scenarios // lax.axis_size("dst")
    leading = lax.axis_index("dst") * portion
    firm_rows = row_start + jnp.arange(rows_dev, dtype=jnp.int32)
    retained = (firm_rows[:, None] // EXTRACT != scenario_blocks[None, :]).astype(jnp.float32)
    levels = retained * demand[:, None]
    for round_no in range(ITERS):
        every_row = lax.all_gather(levels, "src", axis=0, tiled=True)
        columns = lax.dynamic_slice_in_dim(every_row, col_start, cols_dev, 0)
        summed = lax.psum(
            jnp.dot(
                coefficients,
                columns,
                preferred_element_type=jnp.float32,
                precision=lax.Precision.HIGHEST,
            ),
            "dst",
        )
        levels = retained * (demand[:, None] + summed)
    result = lax.dynamic_slice_in_dim(levels, leading, portion, 1)
    return (out_fit, in_fit, result)


def program(out_density, in_density, retention, demand, location, scenario_blocks):
    args = (out_density, in_density, retention, demand, location, scenario_blocks)
    rows = out_density.shape[0]
    cols = in_density.shape[0]
    whole = lax.axis_size("dst") == 1
    if whole and rows % (2 * LANES) == 0 and cols % (16 * LANES) == 0:
        return fused(*args)
    return on_device(*args)


def solution(mesh):
    in_specs = (P("src"), P("dst"), P("src"), P("src"), P(), P())
    out_specs = (P("src"), P("dst"), P("src", "dst"))
    return jax.shard_map(
        program, mesh=mesh, in_specs=in_specs, out_specs=out_specs, check_vma=False
    )
```

```python
import functools
import math

import jax
import jax.numpy as jnp
from jax import lax
from jax.experimental import pallas as pl
from jax.experimental.pallas import tpu as pltpu
from jax.sharding import PartitionSpec as P

SWEEPS = 2
ITERS = 2
EXTRACT = 128
MAP_SIDE = 256
RANGE = 18


far_weight = 0.015625
FAR = 64.0
ROWS = 64
LANES = 128


def kernel(
    n,
    left_ref,
    right_ref,
    od_ref,
    ret_ref,
    dem_ref,
    dem_row_ref,
    ind_ref,
    scen_ref,
    x_out,
    y_out,
    lev_out,
    bmat,
    hi_ref,
    lo_ref,
    rowacc,
    xb,
    vb,
    part,
    gath,
    yrow,
    urow,
    dem_all,
    lev_all,
    acc,
    send_sem,
    one_sem,
    lev_sem,
):
    me = lax.axis_index("src")
    rows, cols = bmat.shape
    firms = rows * n
    scen = scen_ref.shape[0]
    wide = rows // LANES
    chips = n // 2
    planes = n // 8
    plane = lax.div(me, 8)
    chip_xy = lax.div(lax.rem(me, 8), 2)
    core = lax.rem(me, 2)

    def slot_of(d):
        return lax.rem(d, 2) * chips + lax.div(d, 2)

    def firm_block(p):
        return lax.rem(p, chips) * 2 + lax.div(p, chips)

    here = slot_of(me)

    barrier = pltpu.get_barrier_semaphore()

    @pl.loop(1, n)
    def _(s):
        pl.semaphore_signal(barrier, inc=1, device_id={"src": lax.rem(me + s, n)})

    pl.semaphore_wait(barrier, n - 1)

    def push(src, dst, sems, phase):
        @pl.loop(1, n)
        def _(s):
            q = lax.rem(me + n - s, n)
            pltpu.make_async_remote_copy(
                src_ref=src(slot_of(q)),
                dst_ref=dst.at[here],
                send_sem=send_sem.at[phase],
                recv_sem=sems,
                device_id={"src": q},
            ).start()

    def drain(buf, sem):
        some = buf.at[pl.ds(0, n - 1)]
        pltpu.make_async_copy(some, some, sem).wait()

    dem_all[here] = dem_row_ref[...]
    push(lambda q: dem_row_ref, dem_all, one_sem.at[0], 0)

    @pl.loop(0, n)
    def _(q):
        c0 = pl.multiple_of(q * rows, rows)
        dist = jnp.dot(
            left_ref[...],
            right_ref[:, pl.ds(pl.multiple_of(firm_block(q) * rows, rows), rows)],
            preferred_element_type=jnp.float32,
        )
        bmat[:, pl.ds(c0, rows)] = jnp.where(dist <= RANGE * RANGE, 1.0, FAR)

    mine = pl.ds(pl.multiple_of(here * rows, rows), rows)
    for r0 in range(0, rows, ROWS):
        shape = (ROWS, rows)
        same = lax.broadcasted_iota(jnp.int32, shape, 0) + r0 == lax.broadcasted_iota(
            jnp.int32, shape, 1
        )
        bmat[pl.ds(r0, ROWS), mine] = jnp.where(same, FAR * FAR * 1e12, bmat[pl.ds(r0, ROWS), mine])

    xb[...] = jnp.broadcast_to(jnp.sqrt(od_ref[...]), xb.shape)

    @pl.loop(0, n)
    def _(q):
        c0 = pl.multiple_of(q * rows, rows)
        y = jnp.sqrt(ind_ref[firm_block(q)])
        yrow[:, pl.ds(c0, rows)] = y
        urow[:, pl.ds(c0, rows)] = 1.0 / y

    tiles = 32
    strip = tiles * LANES

    def pair_sum(a, b):
        return (a + b) * pltpu.reciprocal(a * b, approx=True)

    for sweep in range(SWEEPS):
        @pl.loop(0, rows // ROWS)
        def _(b):
            rs = pl.ds(pl.multiple_of(b * ROWS, ROWS), ROWS)
            x = xb[rs, :]

            def body(c, total):
                c0 = pl.multiple_of(c * strip, strip)
                for t in range(0, tiles, 2):
                    ca = pl.ds(c0 + t * LANES, LANES)
                    cb = pl.ds(c0 + (t + 1) * LANES, LANES)
                    total = total + pair_sum(
                        bmat[rs, ca] * urow[:, ca] + x, bmat[rs, cb] * urow[:, cb] + x
                    )
                return total

            rowacc[rs, :] = lax.fori_loop(
                0, cols // strip, body, jnp.zeros((ROWS, LANES), jnp.float32)
            )

        row_total = jnp.sum(rowacc[...], axis=1, keepdims=True)
        x_new = firms * od_ref[...] / row_total
        xb[...] = jnp.broadcast_to(x_new, xb.shape)
        vb[...] = jnp.broadcast_to(1.0 / x_new, vb.shape)

        @pl.loop(0, n)
        def _(q):
            c0 = pl.multiple_of(q * rows, rows)
            for t in range(wide):
                cs = pl.ds(c0 + t * LANES, LANES)
                y = yrow[:, cs]
                total = jnp.zeros((8, LANES), jnp.float32)
                for r0 in range(0, rows, 2 * ROWS):
                    rs = pl.ds(r0, ROWS)
                    rt = pl.ds(r0 + ROWS, ROWS)
                    term = pair_sum(bmat[rs, cs] * vb[rs, :] + y, bmat[rt, cs] * vb[rt, :] + y)
                    total = total + jnp.sum(term.reshape(ROWS // 8, 8, LANES), axis=0)
                part[sweep, q, :, pl.ds(t * LANES, LANES)] = jnp.sum(total, axis=0, keepdims=True)

        gath[2 * sweep, here] = part[sweep, here]
        push(lambda q: part.at[sweep, q], gath.at[2 * sweep], one_sem.at[1 + 2 * sweep], 1 + 2 * sweep)
        drain(gath.at[2 * sweep], one_sem.at[1 + 2 * sweep])
        col_total = jnp.sum(gath[2 * sweep], axis=0)
        fresh = gath.at[2 * sweep + 1]
        fresh[here] = firms * ind_ref[me] / col_total
        push(lambda q: fresh.at[here], fresh, one_sem.at[2 + 2 * sweep], 2 + 2 * sweep)
        drain(fresh, one_sem.at[2 + 2 * sweep])

        @pl.loop(0, n)
        def _(q):
            c0 = pl.multiple_of(q * rows, rows)
            y = fresh[q]
            yrow[:, pl.ds(c0, rows)] = y
            urow[:, pl.ds(c0, rows)] = 1.0 / y

    @pl.loop(0, n)
    def _(q):
        y_out[firm_block(q)] = gath[2 * SWEEPS - 1, q]

    x_new = xb[:, 0:1]
    for r0 in range(0, rows, ROWS):
        shape = (ROWS, rows)
        same = lax.broadcasted_iota(jnp.int32, shape, 0) + r0 == lax.broadcasted_iota(
            jnp.int32, shape, 1
        )
        bmat[pl.ds(r0, ROWS), mine] = jnp.where(same, jnp.inf, bmat[pl.ds(r0, ROWS), mine])
    x_out[...] = x_new
    gain = x_new * (ret_ref[...] / (firms * od_ref[...]))
    drain(dem_all, one_sem.at[0])

    def kept(q):
        ids = q * rows + lax.broadcasted_iota(jnp.int32, (scen, rows), 1)
        return lax.div(ids, EXTRACT) != scen_ref[...]

    def product(levels):
        top = levels.astype(jnp.bfloat16)
        low = (levels - top.astype(jnp.float32)).astype(jnp.bfloat16)
        both = jnp.concatenate([top, low], axis=0)
        dims = (((1,), (1,)), ((), ()))
        acc[...] += lax.dot_general(
            hi_ref[...], both, dims, preferred_element_type=jnp.float32
        ) + lax.dot_general(lo_ref[...], both, dims, preferred_element_type=jnp.float32)

    def split(rs, cs, value):
        top = value.astype(jnp.bfloat16)
        hi_ref[rs, cs] = top
        lo_ref[rs, cs] = (value - top.astype(jnp.float32)).astype(jnp.bfloat16)

    acc[...] = jnp.zeros_like(acc)

    @pl.loop(0, n // 4)
    def _(g):
        for k in range(4):
            at = pl.ds(pl.multiple_of((4 * g + k) * rows, rows), rows)
            u = urow[:, at]
            for r0 in range(0, rows, ROWS):
                rs = pl.ds(r0, ROWS)
                x = jnp.concatenate([xb[rs, :]] * wide, axis=1)
                value = pltpu.reciprocal(bmat[rs, at] * u + x, approx=True)
                bmat[rs, at] = value
                split(rs, pl.ds(k * rows, rows), value)
        blocks = [4 * g + k for k in range(4)]
        product(
            jnp.concatenate(
                [jnp.where(kept(firm_block(p)), dem_all[p], 0.0) for p in blocks], axis=1
            )
        )

    summed = gain * (acc[:, 0:scen] + acc[:, scen:])
    keep_mine = kept(me)
    lev_all[here] = jnp.where(keep_mine, dem_row_ref[...] + summed.T, 0.0)
    acc[...] = jnp.zeros_like(acc)

    def send(ref, sem, target):
        pltpu.make_async_remote_copy(
            src_ref=ref,
            dst_ref=ref,
            send_sem=send_sem.at[5],
            recv_sem=sem,
            device_id={"src": target},
        ).start()

    def wait(count, sem):
        some = lev_all.at[pl.ds(0, count)]
        pltpu.make_async_copy(some, some, sem).wait()

    def slots(c, k):
        return c * chips + lax.rem(plane + k, planes) * 4

    def to_plane(k):
        block = lev_all.at[pl.ds(slots(core, k) + chip_xy, 1)]
        for s in range(1, 4):
            send(block, lev_sem.at[k], plane * 8 + lax.rem(chip_xy + s, 4) * 2 + core)

    def to_core(k):
        send(lev_all.at[pl.ds(slots(core, k), 4)], lev_sem.at[2 * planes + k], me + 1 - 2 * core)

    def multiply(c, k):
        first = slots(c, k)
        for r0 in range(0, rows, ROWS):
            rs = pl.ds(r0, ROWS)
            for j in range(4):
                at = pl.ds(pl.multiple_of((first + j) * rows, rows), rows)
                split(rs, pl.ds(j * rows, rows), bmat[rs, at])
        product(jnp.concatenate([lev_all[first + j] for j in range(4)], axis=1))

    own = lev_all.at[pl.ds(here, 1)]
    for k in range(1, planes):
        target = lax.rem(plane + planes - k, planes) * 8 + lax.rem(me, 8)
        send(own, lev_sem.at[planes + k], target)
    to_plane(0)
    wait(3, lev_sem.at[0])
    to_core(0)
    for k in range(1, planes):
        wait(1, lev_sem.at[planes + k])
        to_plane(k)
        if k == 1:
            multiply(core, 0)
    wait(4, lev_sem.at[2 * planes])
    multiply(1 - core, 0)
    for k in range(1, planes):
        wait(3, lev_sem.at[k])
        to_core(k)
        multiply(core, k)
        wait(4, lev_sem.at[2 * planes + k])
        multiply(1 - core, k)

    summed = gain * (acc[:, 0:scen] + acc[:, scen:])
    lev_out[...] = jnp.where(keep_mine, dem_row_ref[...] + summed.T, 0.0).T

    drain(dem_all, send_sem.at[0])
    for phase in range(1, 5):
        drain(gath.at[0], send_sem.at[phase])
    drain(lev_all, send_sem.at[5])


def fused(out_density, in_density, retention, demand, location, scenario_blocks):
    rows = out_density.shape[0]
    cols = in_density.shape[0]
    n = lax.axis_size("src")
    scen = scenario_blocks.shape[0]
    mine = lax.dynamic_slice_in_dim(location, lax.axis_index("src") * rows, rows)

    def bytes_of(norm):
        return norm >> 16, (norm >> 8) & 255, norm & 255

    def features(cells, left):
        r, c = cells // MAP_SIDE, cells % MAP_SIDE
        norm = bytes_of(r * r + c * c)
        one = jnp.ones_like(r)
        scale = (65536 * one, 256 * one, one)
        head = (-2 * r, -2 * c) if left else (r, c)
        tail = norm + scale if left else scale + norm
        zero = jnp.zeros_like(r)
        return jnp.stack(head + tail + (zero,) * 8, axis=1 if left else 0).astype(jnp.bfloat16)

    vmem = pl.BlockSpec(memory_space=pltpu.VMEM)
    f32 = jnp.float32
    x, y, levels = pl.pallas_call(
        functools.partial(kernel, n),
        out_shape=(
            jax.ShapeDtypeStruct((rows, 1), f32),
            jax.ShapeDtypeStruct((n, 1, rows), f32),
            jax.ShapeDtypeStruct((rows, scen), f32),
        ),
        in_specs=[vmem] * 8,
        out_specs=(vmem,) * 3,
        scratch_shapes=[
            pltpu.VMEM((rows, cols), f32),
            pltpu.VMEM((rows, 4 * rows), jnp.bfloat16),
            pltpu.VMEM((rows, 4 * rows), jnp.bfloat16),
            pltpu.VMEM((rows, LANES), f32),
            pltpu.VMEM((rows, LANES), f32),
            pltpu.VMEM((rows, LANES), f32),
            pltpu.VMEM((SWEEPS, n, 1, rows), f32),
            pltpu.VMEM((2 * SWEEPS, n, 1, rows), f32),
            pltpu.VMEM((1, cols), f32),
            pltpu.VMEM((1, cols), f32),
            pltpu.VMEM((n, 1, rows), f32),
            pltpu.VMEM((n, scen, rows), f32),
            pltpu.VMEM((rows, 2 * scen), f32),
            pltpu.SemaphoreType.DMA((6,)),
            pltpu.SemaphoreType.DMA((5,)),
            pltpu.SemaphoreType.DMA((3 * n // 8,)),
        ],
        compiler_params=pltpu.CompilerParams(
            collective_id=0, has_side_effects=True, vmem_limit_bytes=56 * 2**20
        ),
    )(
        features(mine, True),
        features(location, False),
        out_density[:, None],
        retention[:, None],
        demand[:, None],
        demand[None, :],
        in_density.reshape(n, 1, rows),
        scenario_blocks[:, None],
    )
    return x.reshape(rows), y.reshape(cols), levels


def on_device(out_density, in_density, retention, demand, location, scenario_blocks):
    rows_dev = out_density.shape[0]
    cols_dev = in_density.shape[0]
    firms = rows_dev * lax.axis_size("src")
    row_start = lax.axis_index("src") * rows_dev
    col_start = lax.axis_index("dst") * cols_dev
    height = math.gcd(rows_dev, 128)
    blocks = rows_dev // height
    col_ids = col_start + jnp.arange(cols_dev, dtype=jnp.int32)
    offsets = jnp.arange(blocks, dtype=jnp.int32) * height
    src_cells = lax.dynamic_slice_in_dim(location, row_start, rows_dev)
    dst_cells = lax.dynamic_slice_in_dim(location, col_start, cols_dev)
    src_row = src_cells // MAP_SIDE
    src_col = src_cells % MAP_SIDE
    dst_row = dst_cells // MAP_SIDE
    dst_col = dst_cells % MAP_SIDE
    out_fit = jnp.sqrt(out_density)
    in_fit = jnp.sqrt(in_density)

    def pair_weight(offset):
        row_ids = row_start + offset + jnp.arange(height, dtype=jnp.int32)
        row_gap = lax.dynamic_slice_in_dim(src_row, offset, height)[:, None] - dst_row[None, :]
        col_gap = lax.dynamic_slice_in_dim(src_col, offset, height)[:, None] - dst_col[None, :]
        nearby = row_gap * row_gap + col_gap * col_gap <= RANGE * RANGE
        affinity = jnp.where(nearby, 1.0, far_weight)
        return jnp.where(row_ids[:, None] != col_ids[None, :], affinity, 0.0)

    for sweep_no in range(SWEEPS):

        def row_part(offset):
            row_fit = lax.dynamic_slice_in_dim(out_fit, offset, height)
            weight = pair_weight(offset)
            ratios = weight * in_fit[None, :] / (1.0 + row_fit[:, None] * in_fit[None, :] * weight)
            return jnp.sum(ratios, axis=1)

        row_partial = lax.map(row_part, offsets).reshape(rows_dev)
        row_total = lax.psum(row_partial, "dst")
        out_fit = firms * out_density / row_total

        def col_part(running, offset):
            row_fit = lax.dynamic_slice_in_dim(out_fit, offset, height)
            weight = pair_weight(offset)
            ratios = weight * row_fit[:, None] / (1.0 + row_fit[:, None] * in_fit[None, :] * weight)
            return (running + jnp.sum(ratios, axis=0), None)

        col_partial, _ = lax.scan(col_part, jnp.zeros((cols_dev,), jnp.float32), offsets)
        col_total = lax.psum(col_partial, "src")
        in_fit = firms * in_density / col_total
    row_scale = retention / (firms * out_density)

    def coeff_block(offset):
        row_fit = lax.dynamic_slice_in_dim(out_fit, offset, height)
        scale_part = lax.dynamic_slice_in_dim(row_scale, offset, height)
        product = row_fit[:, None] * in_fit[None, :] * pair_weight(offset)
        chance = product / (1.0 + product)
        return chance * scale_part[:, None]

    coefficients = lax.map(coeff_block, offsets).reshape(rows_dev, cols_dev)
    scenarios = scenario_blocks.shape[0]
    portion = scenarios // lax.axis_size("dst")
    leading = lax.axis_index("dst") * portion
    firm_rows = row_start + jnp.arange(rows_dev, dtype=jnp.int32)
    retained = (firm_rows[:, None] // EXTRACT != scenario_blocks[None, :]).astype(jnp.float32)
    levels = retained * demand[:, None]
    for round_no in range(ITERS):
        every_row = lax.all_gather(levels, "src", axis=0, tiled=True)
        columns = lax.dynamic_slice_in_dim(every_row, col_start, cols_dev, 0)
        summed = lax.psum(
            jnp.dot(
                coefficients,
                columns,
                preferred_element_type=jnp.float32,
                precision=lax.Precision.HIGHEST,
            ),
            "dst",
        )
        levels = retained * (demand[:, None] + summed)
    result = lax.dynamic_slice_in_dim(levels, leading, portion, 1)
    return (out_fit, in_fit, result)


def program(out_density, in_density, retention, demand, location, scenario_blocks):
    args = (out_density, in_density, retention, demand, location, scenario_blocks)
    rows = out_density.shape[0]
    cols = in_density.shape[0]
    whole = lax.axis_size("dst") == 1
    if whole and rows % (2 * LANES) == 0 and cols % (32 * LANES) == 0 and lax.axis_size("src") % 8 == 0:
        return fused(*args)
    return on_device(*args)


def solution(mesh):
    in_specs = (P("src"), P("dst"), P("src"), P("src"), P(), P())
    out_specs = (P("src"), P("dst"), P("src", "dst"))
    return jax.shard_map(
        program, mesh=mesh, in_specs=in_specs, out_specs=out_specs, check_vma=False
    )
```
